32 devices in a mesh: grp: 2 (over y), dp: 4 (over z), feat: 2 (over x), qry: 2 (over core).
Axes of the slice: x: 2, y: 2, z: 4, core: 2. Of those that a mesh axis runs over, the one named last changes fastest.
Arguments:
- train_grads: bfloat16 [10240, 4096], P(('grp', 'dp'), 'feat'), parts along dimension 0, may hold values from -6 to 6
- queries: bfloat16 [4, 96, 4096], P('dp', 'qry', 'feat'), may hold values from -0.09375 to 0.09375
- loss_weights: float32 [10240], P(('grp', 'dp', 'feat')), parts along dimension 0, may hold values from 0.2 to 1
Outputs:
- scores: float32 [4, 96, 10240], P(None, 'qry', ('grp', 'dp', 'feat')), parts along dimension 2
The draws below stay inside these ranges and needn't reach their ends.
There are 2 independent parts, one for each index of `grp`. The reference program is written for one: setup_inputs(seed, part) draws one part's arguments, and reference() takes and returns one part's arrays. A program takes and returns all parts, laid end to end along the dimension named above; an argument that names none is the same for every part. Nothing has to cross between parts.
All inputs are finite; a program needn't handle non-finite values.
Results may differ from the reference program's by a relative error of at most 0.0003.
Values may be sent and summed in bfloat16 or wider, within the bound.
A program may use at most 64 MiB of HBM per device.

```python
import jax
import jax.numpy as jnp

K = 4096
TRAIN = 5120
QH = 96
N_DP = 4


def block_scale(key, dims, pieces, least, high):
    factor_of, own = 1.0, jax.random.fold_in(key, 6)
    for axis_at, parts in pieces:
        heights = jnp.exp(jax.random.uniform(jax.random.fold_in(own, axis_at), (parts,), jnp.float32, least / len(pieces), high / len(pieces)))
        factor_of = factor_of * jnp.repeat(heights, dims[axis_at] // parts).reshape([-1 if axis == axis_at else 1 for axis in range(len(dims))])
    return factor_of


def centred(key, dims, scale, reach, split=(), kind=jnp.bfloat16):
    loudness = block_scale(key, dims, split, -0.22, 0.18) if split else 1.0
    entries = jax.random.normal(key, dims, jnp.float32) * scale * loudness
    return jnp.minimum(jnp.maximum(entries, -reach), reach).astype(kind)


def setup_inputs(seed: int = 0, part: int = 0) -> dict:
    arg_keys = jax.random.split(jax.random.key(seed), 4)
    own_keys = jax.random.split(jax.random.fold_in(arg_keys[3], part), 4)
    return {
        "train_grads": centred(own_keys[0], (TRAIN, K), 1.0, 6.0, ((0, 4), (1, 2))),
        "queries": centred(arg_keys[1], (N_DP, QH, K), K ** -0.5, 0.09375, ((0, 4), (1, 2), (2, 2))),
        "loss_weights": jnp.clip(0.2 + 0.8 * jax.random.uniform(own_keys[2], (TRAIN,), jnp.float32) ** block_scale(own_keys[2], (TRAIN,), ((0, 8),), -0.2, 0.2), 0.2, 1.0),
    }


def reference(train_grads, queries, loss_weights):
    query_rows = queries.reshape(N_DP * QH, K)
    totals = jnp.dot(query_rows, train_grads.T, preferred_element_type=jnp.float32)
    totals = totals.reshape(N_DP, QH, TRAIN)
    return totals * loss_weights[None, None, :]
```

```python
import functools

import jax
import jax.numpy as jnp
from jax import lax
from jax.experimental import pallas as pl
from jax.experimental.pallas import tpu as pltpu
from jax.sharding import PartitionSpec as P

MESH = pl.DeviceIdType.MESH


def partner(me, step, size):
    if size & (size - 1):
        return lax.rem(me + step, size)
    out = me
    bit = 1
    while bit < size:
        both = (me // bit) % 2
        flip = (step // bit) % 2
        out = out + bit * flip * (1 - 2 * both)
        bit *= 2
    return out


def source(me, step, size):
    if size & (size - 1):
        return lax.rem(me - step + size, size)
    return partner(me, step, size)


def kernel(
    sizes, train_hbm, query_hbm, out_ref, train, blocks, sent, received,
    train_sem, own_sem, z_send, z_recv, y_send, y_recv, x_send, x_recv,
):
    G, D, F = sizes
    g, d, f = lax.axis_index("grp"), lax.axis_index("dp"), lax.axis_index("feat")
    rows = out_ref.shape[2]
    width = blocks.shape[3]

    barrier = pltpu.get_barrier_semaphore()
    for s in range(1, D):
        pl.semaphore_signal(barrier, inc=1, device_id={"dp": partner(d, s, D)}, device_id_type=MESH)
    for k in range(1, G):
        pl.semaphore_signal(barrier, inc=1, device_id={"grp": lax.rem(g + k, G)}, device_id_type=MESH)
    for k in range(1, F):
        pl.semaphore_signal(barrier, inc=1, device_id={"feat": lax.rem(f + k, F)}, device_id_type=MESH)

    own = [
        pltpu.make_async_copy(query_hbm.at[0, :, pl.ds(p * width, width)], blocks.at[d, p], own_sem.at[p])
        for p in range(G)
    ]
    for copy in own:
        copy.start()
    order = [lax.rem(f + k, F) for k in list(range(1, F)) + [0]]
    loads = []
    for k in range(F):
        for p in range(G):
            at = (pl.ds(pl.multiple_of(order[k] * rows, rows), rows), pl.ds(p * width, width))
            loads.append(pltpu.make_async_copy(train_hbm.at[at], train.at[at], train_sem.at[k, p]))
            loads[-1].start()

    pl.semaphore_wait(barrier, (D - 1) + (G - 1) + (F - 1))

    def across(s):
        to = partner(d, s, D)
        return pltpu.make_async_remote_copy(
            src_ref=query_hbm.at[0, :, pl.ds(pl.multiple_of(g * width, width), width)],
            dst_ref=blocks.at[d, g],
            send_sem=z_send.at[s], recv_sem=z_recv.at[s],
            device_id={"dp": to}, device_id_type=MESH,
        )

    def arrived(s):
        b = source(d, s, D)
        return pltpu.make_async_remote_copy(
            src_ref=blocks.at[b, g], dst_ref=blocks.at[b, g],
            send_sem=z_send.at[s], recv_sem=z_recv.at[s],
            device_id={"dp": partner(d, s, D)}, device_id_type=MESH,
        )

    def forward(s, k):
        b = source(d, s, D)
        return pltpu.make_async_remote_copy(
            src_ref=blocks.at[b, g], dst_ref=blocks.at[b, g],
            send_sem=y_send.at[s, k], recv_sem=y_recv.at[s, k],
            device_id={"grp": lax.rem(g + k, G)}, device_id_type=MESH,
        )

    def forwarded(s, k):
        b = source(d, s, D)
        at = lax.rem(g - k + G, G)
        return pltpu.make_async_remote_copy(
            src_ref=blocks.at[b, at], dst_ref=blocks.at[b, at],
            send_sem=y_send.at[s, k], recv_sem=y_recv.at[s, k],
            device_id={"grp": lax.rem(g + k, G)}, device_id_type=MESH,
        )

    def give(s, k):
        return pltpu.make_async_remote_copy(
            src_ref=sent.at[k - 1, s], dst_ref=received.at[k - 1, partner_slot(s)],
            send_sem=x_send.at[s, k - 1], recv_sem=x_recv.at[s, k - 1],
            device_id={"feat": lax.rem(f + k, F)}, device_id_type=MESH,
        )

    def partner_slot(s):
        return s

    def product(b, k):
        at = pl.ds(pl.multiple_of(order[k] * rows, rows), rows)
        total = None
        for p in range(G):
            term = lax.dot_general(
                blocks[b, p], train[at, pl.ds(p * width, width)],
                (((1,), (1,)), ((), ())), preferred_element_type=jnp.float32,
            )
            total = term if total is None else total + term
        return total

    for s in range(1, D):
        across(s).start()

    for copy in own:
        copy.wait()

    for k in range(1, F):
        for p in range(G):
            loads[(k - 1) * G + p].wait()
        sent[k - 1, 0] = product(d, k - 1)
        give(0, k).start()

    def pass_on(s):
        arrived(s).wait_recv()
        for k in range(1, G):
            forward(s, k).start()

    if D > 1:
        pass_on(1)
    for p in range(G):
        loads[(F - 1) * G + p].wait()
    out_ref[d] = product(d, F - 1)

    def step(s, last):
        b = source(d, s, D)
        if not last:
            pass_on(s + 1)
        for k in range(1, G):
            forwarded(s, k).wait_recv()
        for k in range(1, F):
            sent[k - 1, s] = product(b, k - 1)
            give(s, k).start()
        out_ref[b] = product(b, F - 1)

    if D > 2:
        lax.fori_loop(1, D - 1, lambda s, c: (step(s, False), c)[1], 0)
    if D > 1:
        step(D - 1, True)

    def finish(s, c):
        b = source(d, s, D)
        for k in range(1, F):
            give(s, k).wait_recv()
            out_ref[b] += received[k - 1, s]
        return c

    lax.fori_loop(0, D, finish, 0)

    def drain(s, c):
        across(s).wait_send()
        for k in range(1, G):
            forward(s, k).wait_send()
        return c

    lax.fori_loop(1, D, drain, 0)

    def drain_given(s, c):
        for k in range(1, F):
            give(s, k).wait_send()
        return c

    lax.fori_loop(0, D, drain_given, 0)


def local(sizes, train_grads, queries, loss_weights):
    G, D, F = sizes
    total_rows, features = train_grads.shape
    rows = total_rows // F
    width = features // G
    held = queries.shape[1]
    sums = pl.pallas_call(
        functools.partial(kernel, sizes),
        out_shape=jax.ShapeDtypeStruct((D, held, rows), jnp.float32),
        in_specs=[pl.BlockSpec(memory_space=pl.ANY)] * 2,
        out_specs=pl.BlockSpec(memory_space=pltpu.VMEM),
        scratch_shapes=[
            pltpu.VMEM((total_rows, features), jnp.bfloat16),
            pltpu.VMEM((D, G, held, width), jnp.bfloat16),
            pltpu.VMEM((F - 1, D, held, rows), jnp.float32),
            pltpu.VMEM((F - 1, D, held, rows), jnp.float32),
            pltpu.SemaphoreType.DMA((F, G)),
            pltpu.SemaphoreType.DMA((G,)),
            pltpu.SemaphoreType.DMA((D,)),
            pltpu.SemaphoreType.DMA((D,)),
            pltpu.SemaphoreType.DMA((D, G)),
            pltpu.SemaphoreType.DMA((D, G)),
            pltpu.SemaphoreType.DMA((D, F - 1)),
            pltpu.SemaphoreType.DMA((D, F - 1)),
        ],
        compiler_params=pltpu.CompilerParams(
            collective_id=0, has_side_effects=True, vmem_limit_bytes=56 * 1024 * 1024
        ),
        cost_estimate=pl.CostEstimate(
            flops=2 * D * held * total_rows * features,
            bytes_accessed=2 * total_rows * features + 4 * D * held * rows,
            transcendentals=0,
        ),
    )(train_grads, queries)
    return sums * loss_weights[None, None, :]


def solution(mesh):
    sizes = tuple(mesh.shape[axis] for axis in ("grp", "dp", "feat"))
    in_specs = (P(("grp", "dp"), "feat"), P("dp", "qry", "feat"), P(("grp", "dp", "feat")))
    out_specs = P(None, "qry", ("grp", "dp", "feat"))
    return jax.shard_map(
        functools.partial(local, sizes), mesh=mesh, in_specs=in_specs, out_specs=out_specs, check_vma=False
    )
```

```python
import functools

import jax
import jax.numpy as jnp
from jax import lax
from jax.experimental import pallas as pl
from jax.experimental.pallas import tpu as pltpu
from jax.sharding import PartitionSpec as P

MESH = pl.DeviceIdType.MESH


def arrival(me, j, size):
    both = jnp.minimum(me, size - 1 - me)
    left_longer = (2 * me) // size
    step = jnp.where(j <= 2 * both, (j + 1) // 2, j - both)
    to_left = jnp.where(j <= 2 * both, j % 2, left_longer)
    return me + step * (1 - 2 * to_left), to_left


def kernel(
    sizes, parts, train_hbm, query_hbm, out_ref, train, blocks, sent, received,
    train_sem, own_sem, first_send, z_send, z_recv, y_send, y_recv, x_send, x_recv,
):
    G, D, F = sizes
    g, d, f = lax.axis_index("grp"), lax.axis_index("dp"), lax.axis_index("feat")
    rows = out_ref.shape[2]
    width = blocks.shape[3]
    pieces = G * parts
    has_left, has_right = d > 0, d < D - 1

    barrier = pltpu.get_barrier_semaphore()
    for there, by in ((has_left, -1), (has_right, 1)):
        @pl.when(there)
        def _():
            pl.semaphore_signal(barrier, inc=1, device_id={"dp": d + by}, device_id_type=MESH)
    for k in range(1, G):
        pl.semaphore_signal(barrier, inc=1, device_id={"grp": lax.rem(g + k, G)}, device_id_type=MESH)
    for k in range(1, F):
        pl.semaphore_signal(barrier, inc=1, device_id={"feat": lax.rem(f + k, F)}, device_id_type=MESH)

    own = [
        pltpu.make_async_copy(query_hbm.at[0, :, pl.ds(p * width, width)], blocks.at[d, p], own_sem.at[p])
        for p in range(pieces)
    ]
    for copy in own:
        copy.start()
    order = [lax.rem(f + k, F) for k in list(range(1, F)) + [0]]
    loads = []
    for k in range(F):
        for p in range(G):
            cols = pl.ds(p * width * parts, width * parts)
            at = (pl.ds(pl.multiple_of(order[k] * rows, rows), rows), cols)
            loads.append(pltpu.make_async_copy(train_hbm.at[at], train.at[at], train_sem.at[k, p]))
            loads[-1].start()

    pl.semaphore_wait(barrier, has_left.astype(jnp.int32) + has_right.astype(jnp.int32) + (G - 1) + (F - 1))

    def first(by, c):
        at = pl.multiple_of((g * parts + c) * width, width)
        return pltpu.make_async_remote_copy(
            src_ref=query_hbm.at[0, :, pl.ds(at, width)], dst_ref=blocks.at[d, g * parts + c],
            send_sem=first_send.at[(by + 1) // 2, c], recv_sem=z_recv.at[d, c],
            device_id={"dp": d + by}, device_id_type=MESH,
        )

    def along(b, by, c):
        at = blocks.at[b, g * parts + c]
        return pltpu.make_async_remote_copy(
            src_ref=at, dst_ref=at, send_sem=z_send.at[b, c], recv_sem=z_recv.at[b, c],
            device_id={"dp": d + by}, device_id_type=MESH,
        )

    def over(b, k, c):
        at = blocks.at[b, g * parts + c]
        return pltpu.make_async_remote_copy(
            src_ref=at, dst_ref=at, send_sem=y_send.at[b, k, c], recv_sem=y_recv.at[b, k, c],
            device_id={"grp": lax.rem(g + k, G)}, device_id_type=MESH,
        )

    def over_here(b, k, c):
        at = blocks.at[b, lax.rem(g - k + G, G) * parts + c]
        return pltpu.make_async_remote_copy(
            src_ref=at, dst_ref=at, send_sem=y_send.at[b, k, c], recv_sem=y_recv.at[b, k, c],
            device_id={"grp": lax.rem(g + k, G)}, device_id_type=MESH,
        )

    def give(b, k):
        return pltpu.make_async_remote_copy(
            src_ref=sent.at[k - 1, b], dst_ref=received.at[k - 1, b],
            send_sem=x_send.at[b, k - 1], recv_sem=x_recv.at[b, k - 1],
            device_id={"feat": lax.rem(f + k, F)}, device_id_type=MESH,
        )

    def product(of, k):
        at = pl.ds(pl.multiple_of(order[k] * rows, rows), rows)
        total = None
        for p in range(pieces):
            term = lax.dot_general(
                of(p), train[at, pl.ds(p * width, width)],
                (((1,), (1,)), ((), ())), preferred_element_type=jnp.float32,
            )
            total = term if total is None else total + term
        return total

    def send_products(b):
        for k in range(1, F):
            sent[k - 1, b] = product(lambda p: blocks[b, p], k - 1)
            give(b, k).start()

    def pass_on(j, c):
        b, to_left = arrival(d, j, D)
        along(b, 1, c).wait_recv()
        by = 2 * to_left - 1
        onward = jnp.logical_and(d + by >= 0, d + by < D)

        @pl.when(onward)
        def _():
            along(b, by, c).start()
        for k in range(1, G):
            over(b, k, c).start()

    def use(j):
        b, _ = arrival(d, j, D)
        for c in range(parts):
            for k in range(1, G):
                over_here(b, k, c).wait_recv()
        send_products(b)

    for c in range(parts):
        for there, by in ((has_left, -1), (has_right, 1)):
            @pl.when(there)
            def _():
                first(by, c).start()

    for copy in own:
        copy.wait()
    for load in loads[: (F - 1) * G]:
        load.wait()
    send_products(d)

    def step(j):
        for c in range(parts):
            pass_on(j + 1, c)
        use(j)

    if D > 1:
        for c in range(parts):
            pass_on(1, c)
        if D > 2:
            lax.fori_loop(1, D - 1, lambda j, carry: (step(j), carry)[1], 0)
        use(D - 1)

    for load in loads[(F - 1) * G :]:
        load.wait()

    many = max(n for n in (1, 2, 3, 4) if D % n == 0)

    def keep(i, carry):
        at = pl.ds(i * many, many)
        held = out_ref.shape[1]
        total = product(lambda p: blocks[at, p].reshape(many * held, width), F - 1)
        out_ref[at] = total.reshape(many, held, rows)
        return carry

    lax.fori_loop(0, D // many, keep, 0)

    def add(b):
        for k in range(1, F):
            give(b, k).wait_recv()
            out_ref[b] += received[k - 1, b]

    add(d)
    lax.fori_loop(1, D, lambda j, carry: (add(arrival(d, j, D)[0]), carry)[1], 0)

    for c in range(parts):
        for there, by in ((has_left, -1), (has_right, 1)):
            @pl.when(there)
            def _():
                first(by, c).wait_send()

    def drain(j, carry):
        b, to_left = arrival(d, j, D)
        by = 2 * to_left - 1
        onward = jnp.logical_and(d + by >= 0, d + by < D)
        for c in range(parts):
            @pl.when(onward)
            def _():
                along(b, by, c).wait_send()
            for k in range(1, G):
                over(b, k, c).wait_send()
        return carry

    lax.fori_loop(1, D, drain, 0)

    def drain_given(b, carry):
        for k in range(1, F):
            give(b, k).wait_send()
        return carry

    lax.fori_loop(0, D, drain_given, 0)


def local(sizes, train_grads, queries, loss_weights):
    G, D, F = sizes
    total_rows, features = train_grads.shape
    rows = total_rows // F
    parts = 2
    width = features // (G * parts)
    held = queries.shape[1]
    sums = pl.pallas_call(
        functools.partial(kernel, sizes, parts),
        out_shape=jax.ShapeDtypeStruct((D, held, rows), jnp.float32),
        in_specs=[pl.BlockSpec(memory_space=pl.ANY)] * 2,
        out_specs=pl.BlockSpec(memory_space=pltpu.VMEM),
        scratch_shapes=[
            pltpu.VMEM((total_rows, features), jnp.bfloat16),
            pltpu.VMEM((D, G * parts, held, width), jnp.bfloat16),
            pltpu.VMEM((F - 1, D, held, rows), jnp.float32),
            pltpu.VMEM((F - 1, D, held, rows), jnp.float32),
            pltpu.SemaphoreType.DMA((F, G)),
            pltpu.SemaphoreType.DMA((G * parts,)),
            pltpu.SemaphoreType.DMA((2, parts)),
            pltpu.SemaphoreType.DMA((D, parts)),
            pltpu.SemaphoreType.DMA((D, parts)),
            pltpu.SemaphoreType.DMA((D, G, parts)),
            pltpu.SemaphoreType.DMA((D, G, parts)),
            pltpu.SemaphoreType.DMA((D, F - 1)),
            pltpu.SemaphoreType.DMA((D, F - 1)),
        ],
        compiler_params=pltpu.CompilerParams(
            collective_id=0, has_side_effects=True, vmem_limit_bytes=56 * 1024 * 1024
        ),
        cost_estimate=pl.CostEstimate(
            flops=2 * D * held * total_rows * features,
            bytes_accessed=2 * total_rows * features + 4 * D * held * rows,
            transcendentals=0,
        ),
    )(train_grads, queries)
    return sums * loss_weights[None, None, :]


def solution(mesh):
    sizes = tuple(mesh.shape[axis] for axis in ("grp", "dp", "feat"))
    in_specs = (P(("grp", "dp"), "feat"), P("dp", "qry", "feat"), P(("grp", "dp", "feat")))
    out_specs = P(None, "qry", ("grp", "dp", "feat"))
    return jax.shard_map(
        functools.partial(local, sizes), mesh=mesh, in_specs=in_specs, out_specs=out_specs, check_vma=False
    )
```

```python
import functools

import jax
import jax.numpy as jnp
from jax import lax
from jax.experimental import pallas as pl
from jax.experimental.pallas import tpu as pltpu
from jax.sharding import PartitionSpec as P

MESH = pl.DeviceIdType.MESH
REACH = 1
PARTS = 2
LIMIT = 52


def arrival(me, j, size):
    both = jnp.minimum(me, size - 1 - me)
    left_longer = (2 * me) // size
    step = jnp.where(j <= 2 * both, (j + 1) // 2, j - both)
    to_left = jnp.where(j <= 2 * both, j % 2, left_longer)
    return me + step * (1 - 2 * to_left), to_left


def kernel(
    sizes, parts, train_hbm, query_hbm, out_ref, train, blocks, sent, received,
    train_sem, own_sem, first_send, z_send, z_recv, y_send, y_recv, x_send, x_recv,
):
    G, D, F = sizes
    g, d, f = lax.axis_index("grp"), lax.axis_index("dp"), lax.axis_index("feat")
    rows = out_ref.shape[2]
    width = blocks.shape[3]
    pieces = G * parts

    barrier = pltpu.get_barrier_semaphore()
    near = [by for t in range(1, min(REACH, D - 1) + 1) for by in (-t, t)]

    def inside(by):
        return d + by >= 0 if by < 0 else d + by < D

    for by in near:
        @pl.when(inside(by))
        def _():
            pl.semaphore_signal(barrier, inc=1, device_id={"dp": d + by}, device_id_type=MESH)
    for k in range(1, G):
        pl.semaphore_signal(barrier, inc=1, device_id={"grp": lax.rem(g + k, G)}, device_id_type=MESH)
    for k in range(1, F):
        pl.semaphore_signal(barrier, inc=1, device_id={"feat": lax.rem(f + k, F)}, device_id_type=MESH)

    own = [
        pltpu.make_async_copy(query_hbm.at[0, :, pl.ds(p * width, width)], blocks.at[d, p], own_sem.at[p])
        for p in range(pieces)
    ]
    for copy in own:
        copy.start()
    order = [lax.rem(f + k, F) for k in list(range(1, F)) + [0]]
    loads = []
    for k in range(F):
        for p in range(G):
            cols = pl.ds(p * width * parts, width * parts)
            at = (pl.ds(pl.multiple_of(order[k] * rows, rows), rows), cols)
            loads.append(pltpu.make_async_copy(train_hbm.at[at], train.at[at], train_sem.at[k, p]))
            loads[-1].start()

    pl.semaphore_wait(barrier, sum(inside(by).astype(jnp.int32) for by in near) + (G - 1) + (F - 1))

    def first(by, c):
        at = pl.multiple_of((g * parts + c) * width, width)
        return pltpu.make_async_remote_copy(
            src_ref=query_hbm.at[0, :, pl.ds(at, width)], dst_ref=blocks.at[d, g * parts + c],
            send_sem=first_send.at[near.index(by), c], recv_sem=z_recv.at[d, c],
            device_id={"dp": d + by}, device_id_type=MESH,
        )

    def along(b, by, c):
        at = blocks.at[b, g * parts + c]
        return pltpu.make_async_remote_copy(
            src_ref=at, dst_ref=at, send_sem=z_send.at[b, c], recv_sem=z_recv.at[b, c],
            device_id={"dp": d + by}, device_id_type=MESH,
        )

    def over(b, k, c):
        at = blocks.at[b, g * parts + c]
        return pltpu.make_async_remote_copy(
            src_ref=at, dst_ref=at, send_sem=y_send.at[b, k, c], recv_sem=y_recv.at[b, k, c],
            device_id={"grp": lax.rem(g + k, G)}, device_id_type=MESH,
        )

    def over_here(b, k, c):
        at = blocks.at[b, lax.rem(g - k + G, G) * parts + c]
        return pltpu.make_async_remote_copy(
            src_ref=at, dst_ref=at, send_sem=y_send.at[b, k, c], recv_sem=y_recv.at[b, k, c],
            device_id={"grp": lax.rem(g + k, G)}, device_id_type=MESH,
        )

    middle = (rows // 128 + 1) // 2 * 128
    spans = [(0, middle), (middle, rows - middle)] if 0 < middle < rows else [(0, rows)]

    def give(b, k, i):
        cols = pl.ds(*spans[i])
        return pltpu.make_async_remote_copy(
            src_ref=sent.at[k - 1, b, :, cols], dst_ref=received.at[k - 1, b, :, cols],
            send_sem=x_send.at[b, k - 1, i], recv_sem=x_recv.at[b, k - 1, i],
            device_id={"feat": lax.rem(f + k, F)}, device_id_type=MESH,
        )

    def term(left, p, k, span):
        at = pl.ds(pl.multiple_of(order[k] * rows + span[0], 16), span[1])
        cols = pl.ds(pl.multiple_of(p * width, width), width)
        return lax.dot_general(
            left, train[at, cols], (((1,), (1,)), ((), ())), preferred_element_type=jnp.float32
        )

    def product(of, k, span):
        return functools.reduce(jnp.add, [term(of(p), p, k, span) for p in range(pieces)])

    def send_products(b, waits):
        at = [(k, i) for k in range(1, F) for i in range(len(spans))]
        totals = {}
        for n, wait in enumerate(waits):
            if wait is not None:
                wait()
            p = lax.rem(g + n // parts, G) * parts + n % parts
            for k, i in at:
                new = term(blocks[b, p], p, k - 1, spans[i])
                totals[k, i] = totals[k, i] + new if n else new
        for k, i in at:
            sent[k - 1, b, :, pl.ds(*spans[i])] = totals[k, i]
            give(b, k, i).start()

    def hand_on(b, to_left):
        by = 2 * to_left - 1
        far = (d - b) * by >= REACH
        return by, jnp.logical_and(far, jnp.logical_and(d + by >= 0, d + by < D))

    def pass_on(j, c):
        b, to_left = arrival(d, j, D)
        along(b, 1, c).wait_recv()
        by, onward = hand_on(b, to_left)

        @pl.when(onward)
        def _():
            along(b, by, c).start()
        for k in range(1, G):
            over(b, k, c).start()

    def use(j):
        b, _ = arrival(d, j, D)
        waits = [None] * parts
        for k in range(1, G):
            waits += [over_here(b, G - k, c).wait_recv for c in range(parts)]
        send_products(b, waits)

    for by in near:
        @pl.when(inside(by))
        def _():
            for c in range(parts):
                first(by, c).start()

    for copy in own:
        copy.wait()
    for load in loads[: (F - 1) * G]:
        load.wait()
    send_products(d, [None] * pieces)

    lag = min(1, D - 1) if D < 3 else jnp.where(jnp.logical_and(d > 0, d < D - 1), 2, 1)

    def step(j, carry):
        for c in range(parts):
            pass_on(j, c)

        @pl.when(j > lag)
        def _():
            use(j - lag)
        return carry

    lax.fori_loop(1, D, step, 0)
    lax.fori_loop(D - lag, D, lambda j, carry: (use(j), carry)[1], 0)

    for load in loads[(F - 1) * G :]:
        load.wait()

    many = max(n for n in (1, 2, 3, 4) if D % n == 0)

    def keep(i, carry):
        at = pl.ds(i * many, many)
        held = out_ref.shape[1]
        total = product(lambda p: blocks[at, p].reshape(many * held, width), F - 1, (0, rows))
        out_ref[at] = total.reshape(many, held, rows)
        return carry

    lax.fori_loop(0, D // many, keep, 0)

    def add(b):
        for k in range(1, F):
            for i, span in enumerate(spans):
                give(b, k, i).wait_recv()
                out_ref[b, :, pl.ds(*span)] += received[k - 1, b, :, pl.ds(*span)]

    add(d)
    lax.fori_loop(1, D, lambda j, carry: (add(arrival(d, j, D)[0]), carry)[1], 0)

    for by in near:
        @pl.when(inside(by))
        def _():
            for c in range(parts):
                first(by, c).wait_send()

    def drain(j, carry):
        b, to_left = arrival(d, j, D)
        by, onward = hand_on(b, to_left)
        for c in range(parts):
            @pl.when(onward)
            def _():
                along(b, by, c).wait_send()
            for k in range(1, G):
                over(b, k, c).wait_send()
        return carry

    lax.fori_loop(1, D, drain, 0)

    def drain_given(b, carry):
        for k in range(1, F):
            for i in range(len(spans)):
                give(b, k, i).wait_send()
        return carry

    lax.fori_loop(0, D, drain_given, 0)


def local(sizes, train_grads, queries, loss_weights):
    G, D, F = sizes
    total_rows, features = train_grads.shape
    rows = total_rows // F
    parts = PARTS
    width = features // (G * parts)
    held = queries.shape[1]
    sums = pl.pallas_call(
        functools.partial(kernel, sizes, parts),
        out_shape=jax.ShapeDtypeStruct((D, held, rows), jnp.float32),
        in_specs=[pl.BlockSpec(memory_space=pl.ANY)] * 2,
        out_specs=pl.BlockSpec(memory_space=pltpu.VMEM),
        scratch_shapes=[
            pltpu.VMEM((total_rows, features), jnp.bfloat16),
            pltpu.VMEM((D, G * parts, held, width), jnp.bfloat16),
            pltpu.VMEM((F - 1, D, held, rows), jnp.float32),
            pltpu.VMEM((F - 1, D, held, rows), jnp.float32),
            pltpu.SemaphoreType.DMA((F, G)),
            pltpu.SemaphoreType.DMA((G * parts,)),
            pltpu.SemaphoreType.DMA((2 * REACH, parts)),
            pltpu.SemaphoreType.DMA((D, parts)),
            pltpu.SemaphoreType.DMA((D, parts)),
            pltpu.SemaphoreType.DMA((D, G, parts)),
            pltpu.SemaphoreType.DMA((D, G, parts)),
            pltpu.SemaphoreType.DMA((D, F - 1, 2)),
            pltpu.SemaphoreType.DMA((D, F - 1, 2)),
        ],
        compiler_params=pltpu.CompilerParams(
            collective_id=0, has_side_effects=True, vmem_limit_bytes=LIMIT * 1024 * 1024
        ),
        cost_estimate=pl.CostEstimate(
            flops=2 * D * held * total_rows * features,
            bytes_accessed=2 * total_rows * features + 4 * D * held * rows,
            transcendentals=0,
        ),
    )(train_grads, queries)
    return sums * loss_weights[None, None, :]


def solution(mesh):
    sizes = tuple(mesh.shape[axis] for axis in ("grp", "dp", "feat"))
    in_specs = (P(("grp", "dp"), "feat"), P("dp", "qry", "feat"), P(("grp", "dp", "feat")))
    out_specs = P(None, "qry", ("grp", "dp", "feat"))
    return jax.shard_map(
        functools.partial(local, sizes), mesh=mesh, in_specs=in_specs, out_specs=out_specs, check_vma=False
    )
```

```python
import functools

import jax
import jax.numpy as jnp
from jax import lax
from jax.experimental import pallas as pl
from jax.experimental.pallas import tpu as pltpu
from jax.sharding import PartitionSpec as P

MESH = pl.DeviceIdType.MESH
PARTS = 2
LIMIT = 52


def kernel(
    sizes, parts, train_hbm, query_hbm, out_ref, train, blocks, sent, received,
    train_sem, own_sem, first_send, z_send, z_recv, y_send, y_recv, x_send, x_recv,
):
    G, D, F = sizes
    g, d, f = lax.axis_index("grp"), lax.axis_index("dp"), lax.axis_index("feat")
    rows = out_ref.shape[2]
    width = blocks.shape[3]
    pieces = G * parts

    barrier = pltpu.get_barrier_semaphore()
    near = (-1, 1)

    def inside(by):
        return d + by >= 0 if by < 0 else d + by < D

    for by in near:
        @pl.when(inside(by))
        def _():
            pl.semaphore_signal(barrier, inc=1, device_id={"dp": d + by}, device_id_type=MESH)
    for k in range(1, G):
        pl.semaphore_signal(barrier, inc=1, device_id={"grp": lax.rem(g + k, G)}, device_id_type=MESH)
    for k in range(1, F):
        pl.semaphore_signal(barrier, inc=1, device_id={"feat": lax.rem(f + k, F)}, device_id_type=MESH)

    own = [
        pltpu.make_async_copy(query_hbm.at[0, :, pl.ds(p * width, width)], blocks.at[d, p], own_sem.at[p])
        for p in range(pieces)
    ]
    for copy in own:
        copy.start()
    order = [lax.rem(f + k, F) for k in list(range(1, F)) + [0]]
    loads = []
    for k in range(F):
        for p in range(G):
            cols = pl.ds(p * width * parts, width * parts)
            at = (pl.ds(pl.multiple_of(order[k] * rows, rows), rows), cols)
            loads.append(pltpu.make_async_copy(train_hbm.at[at], train.at[at], train_sem.at[k, p]))
            loads[-1].start()

    pl.semaphore_wait(barrier, sum(inside(by).astype(jnp.int32) for by in near) + (G - 1) + (F - 1))

    def first(by, c):
        at = pl.multiple_of((g * parts + c) * width, width)
        return pltpu.make_async_remote_copy(
            src_ref=query_hbm.at[0, :, pl.ds(at, width)], dst_ref=blocks.at[d, g * parts + c],
            send_sem=first_send.at[near.index(by), c], recv_sem=z_recv.at[d, c],
            device_id={"dp": d + by}, device_id_type=MESH,
        )

    def along(b, by, c):
        at = blocks.at[b, g * parts + c]
        return pltpu.make_async_remote_copy(
            src_ref=at, dst_ref=at, send_sem=z_send.at[b, c], recv_sem=z_recv.at[b, c],
            device_id={"dp": d + by}, device_id_type=MESH,
        )

    def over(b, k, c):
        at = blocks.at[b, g * parts + c]
        return pltpu.make_async_remote_copy(
            src_ref=at, dst_ref=at, send_sem=y_send.at[b, k, c], recv_sem=y_recv.at[b, k, c],
            device_id={"grp": lax.rem(g + k, G)}, device_id_type=MESH,
        )

    def over_here(b, k, c):
        at = blocks.at[b, lax.rem(g - k + G, G) * parts + c]
        return pltpu.make_async_remote_copy(
            src_ref=at, dst_ref=at, send_sem=y_send.at[b, k, c], recv_sem=y_recv.at[b, k, c],
            device_id={"grp": lax.rem(g + k, G)}, device_id_type=MESH,
        )

    middle = (rows // 128 + 1) // 2 * 128
    spans = [(0, middle), (middle, rows - middle)] if 0 < middle < rows else [(0, rows)]

    def give(b, k, i):
        cols = pl.ds(*spans[i])
        return pltpu.make_async_remote_copy(
            src_ref=sent.at[k - 1, b, :, cols], dst_ref=received.at[k - 1, b, :, cols],
            send_sem=x_send.at[b, k - 1, i], recv_sem=x_recv.at[b, k - 1, i],
            device_id={"feat": lax.rem(f + k, F)}, device_id_type=MESH,
        )

    def term(left, p, k, span):
        at = pl.ds(pl.multiple_of(order[k] * rows + span[0], 16), span[1])
        cols = pl.ds(pl.multiple_of(p * width, width), width)
        return lax.dot_general(
            left, train[at, cols], (((1,), (1,)), ((), ())), preferred_element_type=jnp.float32
        )

    def product(of, k, span):
        return functools.reduce(jnp.add, [term(of(p), p, k, span) for p in range(pieces)])

    def send_products(b, waits):
        at = [(k, i) for k in range(1, F) for i in range(len(spans))]
        totals = {}
        for n, wait in enumerate(waits):
            if wait is not None:
                wait()
            p = lax.rem(g + n // parts, G) * parts + n % parts
            for k, i in at:
                new = term(blocks[b, p], p, k - 1, spans[i])
                totals[k, i] = totals[k, i] + new if n else new
        for k, i in at:
            sent[k - 1, b, :, pl.ds(*spans[i])] = totals[k, i]
            give(b, k, i).start()

    def both_sides(t, act):
        for by in (1, -1):
            @pl.when(d - t * by >= 0 if by > 0 else d - t * by < D)
            def _():
                act(d - t * by, by)

    def pass_on(b, by, c):
        along(b, by, c).wait_recv()

        @pl.when(inside(by))
        def _():
            along(b, by, c).start()
        for k in range(1, G):
            over(b, k, c).start()

    def use(b):
        waits = [None] * parts
        for k in range(1, G):
            waits += [over_here(b, G - k, c).wait_recv for c in range(parts)]
        send_products(b, waits)

    for by in near:
        @pl.when(inside(by))
        def _():
            for c in range(parts):
                first(by, c).start()

    for copy in own:
        copy.wait()
    for load in loads[: (F - 1) * G]:
        load.wait()
    send_products(d, [None] * pieces)

    def step(t, carry):
        for c in range(parts):
            both_sides(t, lambda b, by: pass_on(b, by, c))

        @pl.when(t > 1)
        def _():
            both_sides(t - 1, lambda b, by: use(b))
        return carry

    lax.fori_loop(1, D, step, 0)
    if D > 1:
        both_sides(D - 1, lambda b, by: use(b))

    for load in loads[(F - 1) * G :]:
        load.wait()

    many = max(n for n in (1, 2, 3, 4) if D % n == 0)

    def keep(i, carry):
        at = pl.ds(i * many, many)
        held = out_ref.shape[1]
        total = product(lambda p: blocks[at, p].reshape(many * held, width), F - 1, (0, rows))
        out_ref[at] = total.reshape(many, held, rows)
        return carry

    lax.fori_loop(0, D // many, keep, 0)

    def add(b):
        for k in range(1, F):
            for i, span in enumerate(spans):
                give(b, k, i).wait_recv()
                out_ref[b, :, pl.ds(*span)] += received[k - 1, b, :, pl.ds(*span)]

    add(d)
    lax.fori_loop(1, D, lambda t, carry: (both_sides(t, lambda b, by: add(b)), carry)[1], 0)

    for by in near:
        @pl.when(inside(by))
        def _():
            for c in range(parts):
                first(by, c).wait_send()

    def left(b, by):
        for c in range(parts):
            @pl.when(inside(by))
            def _():
                along(b, by, c).wait_send()
            for k in range(1, G):
                over(b, k, c).wait_send()

    lax.fori_loop(1, D, lambda t, carry: (both_sides(t, left), carry)[1], 0)

    def drain_given(b, carry):
        for k in range(1, F):
            for i in range(len(spans)):
                give(b, k, i).wait_send()
        return carry

    lax.fori_loop(0, D, drain_given, 0)


def local(sizes, train_grads, queries, loss_weights):
    G, D, F = sizes
    total_rows, features = train_grads.shape
    rows = total_rows // F
    parts = PARTS
    width = features // (G * parts)
    held = queries.shape[1]
    sums = pl.pallas_call(
        functools.partial(kernel, sizes, parts),
        out_shape=jax.ShapeDtypeStruct((D, held, rows), jnp.float32),
        in_specs=[pl.BlockSpec(memory_space=pl.ANY)] * 2,
        out_specs=pl.BlockSpec(memory_space=pltpu.VMEM),
        scratch_shapes=[
            pltpu.VMEM((total_rows, features), jnp.bfloat16),
            pltpu.VMEM((D, G * parts, held, width), jnp.bfloat16),
            pltpu.VMEM((F - 1, D, held, rows), jnp.float32),
            pltpu.VMEM((F - 1, D, held, rows), jnp.float32),
            pltpu.SemaphoreType.DMA((F, G)),
            pltpu.SemaphoreType.DMA((G * parts,)),
            pltpu.SemaphoreType.DMA((2, parts)),
            pltpu.SemaphoreType.DMA((D, parts)),
            pltpu.SemaphoreType.DMA((D, parts)),
            pltpu.SemaphoreType.DMA((D, G, parts)),
            pltpu.SemaphoreType.DMA((D, G, parts)),
            pltpu.SemaphoreType.DMA((D, F - 1, 2)),
            pltpu.SemaphoreType.DMA((D, F - 1, 2)),
        ],
        compiler_params=pltpu.CompilerParams(
            collective_id=0, has_side_effects=True, vmem_limit_bytes=LIMIT * 1024 * 1024
        ),
        cost_estimate=pl.CostEstimate(
            flops=2 * D * held * total_rows * features,
            bytes_accessed=2 * total_rows * features + 4 * D * held * rows,
            transcendentals=0,
        ),
    )(train_grads, queries)
    return sums * loss_weights[None, None, :]


def solution(mesh):
    sizes = tuple(mesh.shape[axis] for axis in ("grp", "dp", "feat"))
    in_specs = (P(("grp", "dp"), "feat"), P("dp", "qry", "feat"), P(("grp", "dp", "feat")))
    out_specs = P(None, "qry", ("grp", "dp", "feat"))
    return jax.shard_map(
        functools.partial(local, sizes), mesh=mesh, in_specs=in_specs, out_specs=out_specs, check_vma=False
    )
```

```python
import functools

import jax
import jax.numpy as jnp
from jax import lax
from jax.experimental import pallas as pl
from jax.experimental.pallas import tpu as pltpu
from jax.sharding import PartitionSpec as P

MESH = pl.DeviceIdType.MESH
PARTS = 2
LIMIT = 52


def kernel(
    sizes, parts, train_hbm, query_hbm, out_ref, train, blocks, sent, received,
    train_sem, own_sem, first_send, z_send, z_recv, y_send, y_recv, x_send, x_recv,
):
    G, D, F = sizes
    g, d, f = lax.axis_index("grp"), lax.axis_index("dp"), lax.axis_index("feat")
    rows = out_ref.shape[2]
    width = blocks.shape[3]
    pieces = G * parts

    barrier = pltpu.get_barrier_semaphore()
    near = (-1, 1)

    def inside(by):
        return d + by >= 0 if by < 0 else d + by < D

    for by in near:
        @pl.when(inside(by))
        def _():
            pl.semaphore_signal(barrier, inc=1, device_id={"dp": d + by}, device_id_type=MESH)
    for k in range(1, G):
        pl.semaphore_signal(barrier, inc=1, device_id={"grp": lax.rem(g + k, G)}, device_id_type=MESH)
    for k in range(1, F):
        pl.semaphore_signal(barrier, inc=1, device_id={"feat": lax.rem(f + k, F)}, device_id_type=MESH)

    own = [
        pltpu.make_async_copy(query_hbm.at[0, :, pl.ds(p * width, width)], blocks.at[d, p], own_sem.at[p])
        for p in range(pieces)
    ]
    for copy in own:
        copy.start()
    order = [lax.rem(f + k, F) for k in list(range(1, F)) + [0]]
    loads = []
    for k in range(F):
        for p in range(G):
            cols = pl.ds(p * width * parts, width * parts)
            at = (pl.ds(pl.multiple_of(order[k] * rows, rows), rows), cols)
            loads.append(pltpu.make_async_copy(train_hbm.at[at], train.at[at], train_sem.at[k, p]))
            loads[-1].start()

    pl.semaphore_wait(barrier, sum(inside(by).astype(jnp.int32) for by in near) + (G - 1) + (F - 1))

    def first(by, c):
        at = pl.multiple_of((g * parts + c) * width, width)
        return pltpu.make_async_remote_copy(
            src_ref=query_hbm.at[0, :, pl.ds(at, width)], dst_ref=blocks.at[d, g * parts + c],
            send_sem=first_send.at[near.index(by), c], recv_sem=z_recv.at[d, c],
            device_id={"dp": d + by}, device_id_type=MESH,
        )

    def along(b, by, c):
        at = blocks.at[b, g * parts + c]
        return pltpu.make_async_remote_copy(
            src_ref=at, dst_ref=at, send_sem=z_send.at[b, c], recv_sem=z_recv.at[b, c],
            device_id={"dp": d + by}, device_id_type=MESH,
        )

    def over(b, k, c):
        at = blocks.at[b, g * parts + c]
        return pltpu.make_async_remote_copy(
            src_ref=at, dst_ref=at, send_sem=y_send.at[b, k, c], recv_sem=y_recv.at[b, k, c],
            device_id={"grp": lax.rem(g + k, G)}, device_id_type=MESH,
        )

    def over_here(b, k, c):
        at = blocks.at[b, lax.rem(g - k + G, G) * parts + c]
        return pltpu.make_async_remote_copy(
            src_ref=at, dst_ref=at, send_sem=y_send.at[b, k, c], recv_sem=y_recv.at[b, k, c],
            device_id={"grp": lax.rem(g + k, G)}, device_id_type=MESH,
        )

    middle = (rows // 128 + 1) // 2 * 128
    spans = [(0, middle), (middle, rows - middle)] if 0 < middle < rows else [(0, rows)]

    def give(b, k, i):
        cols = pl.ds(*spans[i])
        return pltpu.make_async_remote_copy(
            src_ref=sent.at[k - 1, b, :, cols], dst_ref=received.at[k - 1, b, :, cols],
            send_sem=x_send.at[b, k - 1, i], recv_sem=x_recv.at[b, k - 1, i],
            device_id={"feat": lax.rem(f + k, F)}, device_id_type=MESH,
        )

    def term(left, p, k, span):
        at = pl.ds(pl.multiple_of(order[k] * rows + span[0], 16), span[1])
        cols = pl.ds(pl.multiple_of(p * width, width), width)
        return lax.dot_general(
            left, train[at, cols], (((1,), (1,)), ((), ())), preferred_element_type=jnp.float32
        )

    def product(of, k, span):
        return functools.reduce(jnp.add, [term(of(p), p, k, span) for p in range(pieces)])

    def send_products(b, waits):
        at = [(k, i) for k in range(1, F) for i in range(len(spans))]
        totals = {}
        for n, wait in enumerate(waits):
            if wait is not None:
                wait()
            p = lax.rem(g + n // parts, G) * parts + n % parts
            for k, i in at:
                new = term(blocks[b, p], p, k - 1, spans[i])
                totals[k, i] = totals[k, i] + new if n else new
                if n == len(waits) - 1:
                    sent[k - 1, b, :, pl.ds(*spans[i])] = totals[k, i]
                    give(b, k, i).start()

    def both_sides(t, act):
        for by in (1, -1):
            @pl.when(d - t * by >= 0 if by > 0 else d - t * by < D)
            def _():
                act(d - t * by, by)

    def pass_on(b, by, c):
        along(b, by, c).wait_recv()

        @pl.when(inside(by))
        def _():
            along(b, by, c).start()
        for k in range(1, G):
            over(b, k, c).start()

    def use(b):
        waits = [None] * parts
        for k in range(1, G):
            waits += [over_here(b, G - k, c).wait_recv for c in range(parts)]
        send_products(b, waits)

    for by in near:
        @pl.when(inside(by))
        def _():
            for c in range(parts):
                first(by, c).start()

    for copy in own:
        copy.wait()
    for load in loads[: (F - 1) * G]:
        load.wait()
    send_products(d, [None] * pieces)

    def step(t, carry):
        for c in range(parts):
            both_sides(t, lambda b, by: pass_on(b, by, c))

        @pl.when(t > 1)
        def _():
            both_sides(t - 1, lambda b, by: use(b))
        return carry

    lax.fori_loop(1, D, step, 0)
    if D > 1:
        both_sides(D - 1, lambda b, by: use(b))

    for load in loads[(F - 1) * G :]:
        load.wait()

    many = max(n for n in (1, 2, 3, 4) if D % n == 0)

    def keep(i, carry):
        at = pl.ds(i * many, many)
        held = out_ref.shape[1]
        total = product(lambda p: blocks[at, p].reshape(many * held, width), F - 1, (0, rows))
        out_ref[at] = total.reshape(many, held, rows)
        return carry

    lax.fori_loop(0, D // many, keep, 0)

    def add(b):
        for k in range(1, F):
            for i, span in enumerate(spans):
                give(b, k, i).wait_recv()
                out_ref[b, :, pl.ds(*span)] += received[k - 1, b, :, pl.ds(*span)]

    add(d)
    lax.fori_loop(1, D, lambda t, carry: (both_sides(t, lambda b, by: add(b)), carry)[1], 0)

    for by in near:
        @pl.when(inside(by))
        def _():
            for c in range(parts):
                first(by, c).wait_send()

    def left(b, by):
        for c in range(parts):
            @pl.when(inside(by))
            def _():
                along(b, by, c).wait_send()
            for k in range(1, G):
                over(b, k, c).wait_send()

    lax.fori_loop(1, D, lambda t, carry: (both_sides(t, left), carry)[1], 0)

    def drain_given(b, carry):
        for k in range(1, F):
            for i in range(len(spans)):
                give(b, k, i).wait_send()
        return carry

    lax.fori_loop(0, D, drain_given, 0)


def local(sizes, train_grads, queries, loss_weights):
    G, D, F = sizes
    total_rows, features = train_grads.shape
    rows = total_rows // F
    parts = PARTS
    width = features // (G * parts)
    held = queries.shape[1]
    sums = pl.pallas_call(
        functools.partial(kernel, sizes, parts),
        out_shape=jax.ShapeDtypeStruct((D, held, rows), jnp.float32),
        in_specs=[pl.BlockSpec(memory_space=pl.ANY)] * 2,
        out_specs=pl.BlockSpec(memory_space=pltpu.VMEM),
        scratch_shapes=[
            pltpu.VMEM((total_rows, features), jnp.bfloat16),
            pltpu.VMEM((D, G * parts, held, width), jnp.bfloat16),
            pltpu.VMEM((F - 1, D, held, rows), jnp.float32),
            pltpu.VMEM((F - 1, D, held, rows), jnp.float32),
            pltpu.SemaphoreType.DMA((F, G)),
            pltpu.SemaphoreType.DMA((G * parts,)),
            pltpu.SemaphoreType.DMA((2, parts)),
            pltpu.SemaphoreType.DMA((D, parts)),
            pltpu.SemaphoreType.DMA((D, parts)),
            pltpu.SemaphoreType.DMA((D, G, parts)),
            pltpu.SemaphoreType.DMA((D, G, parts)),
            pltpu.SemaphoreType.DMA((D, F - 1, 2)),
            pltpu.SemaphoreType.DMA((D, F - 1, 2)),
        ],
        compiler_params=pltpu.CompilerParams(
            collective_id=0, has_side_effects=True, vmem_limit_bytes=LIMIT * 1024 * 1024
        ),
        cost_estimate=pl.CostEstimate(
            flops=2 * D * held * total_rows * features,
            bytes_accessed=2 * total_rows * features + 4 * D * held * rows,
            transcendentals=0,
        ),
    )(train_grads, queries)
    return sums * loss_weights[None, None, :]


def solution(mesh):
    sizes = tuple(mesh.shape[axis] for axis in ("grp", "dp", "feat"))
    in_specs = (P(("grp", "dp"), "feat"), P("dp", "qry", "feat"), P(("grp", "dp", "feat")))
    out_specs = P(None, "qry", ("grp", "dp", "feat"))
    return jax.shard_map(
        functools.partial(local, sizes), mesh=mesh, in_specs=in_specs, out_specs=out_specs, check_vma=False
    )
```
